256 devices in a mesh: orb: 64 (over y, z, core), rep: 4 (over x).
Axes of the slice: x: 4, y: 4, z: 8, core: 2. Of those that a mesh axis runs over, the one named last changes fastest.
Arguments:
- amplitudes: bfloat16 [4, 2816, 65536], P('rep', 'orb'), may hold values from -6 to 6
- integral_slab: bfloat16 [4, 2816, 8192], P('rep', None, 'orb'), may hold values from -0.0546875 to 0.0546875
- allowed_slots: int32 [8, 11264], P(None, 'rep'), may hold values 0 or 1
- row_energy: float32 [65536], P('orb'), may hold values from 0.5 to 3
- col_energy: float32 [8, 1024], P(None, 'rep'), may hold values from 0.5 to 3
Outputs:
- update: float32 [1024, 65536], P('rep', 'orb')
The draws below stay inside these ranges and needn't reach their ends.
All inputs are finite; a program needn't handle non-finite values. No bound on the sum of `allowed_slots` on one device may be relied on, other than what follows from the above.
Results may differ from the reference program's by a relative error of at most 0.0003.
Values may be sent and summed in bfloat16 or wider, within the bound.
A program may use at most 128 MiB of HBM per device.

```python
import jax
import jax.numpy as jnp
from jax import lax

IRREPS = 8
SLOTS = 11264
SLOTS_PART = 2816
ROWS = 65536
ROWS_IRREP = 8192
COLS_IRREP = 1024
N_REP = 4


def set_ends(entries, rng, least, high):
    extent = entries.shape
    index_at = [jax.random.randint(jax.random.fold_in(rng, axis), (), 0, extent[axis]) for axis in range(len(extent))]
    entries = entries.at[tuple(index_at)].set(least)
    longest = extent.index(max(extent))
    index_at[longest] = (index_at[longest] + 1) % extent[longest]
    return entries.at[tuple(index_at)].set(high)


def level_of(own_key, extent, shards, least, largest):
    def one(dim, shards_of):
        steps = jax.random.uniform(jax.random.fold_in(jax.random.fold_in(own_key, 6), dim), (shards_of,), jnp.float32, least / len(shards), largest / len(shards))
        return jnp.repeat(jnp.exp(steps), extent[dim] // shards_of).reshape((-1,) + (1,) * (len(extent) - dim - 1))

    gain = one(*shards[0])
    for cut in shards[1:]:
        gain = gain * one(*cut)
    return gain


def normal_values(stream_key, extent, spread, limit, cuts=(), dtype=jnp.bfloat16):
    drawn = jax.random.normal(stream_key, extent, jnp.float32) * spread
    if len(cuts) > 0:
        drawn = level_of(stream_key, extent, cuts, -0.22, 0.18) * drawn
    return jnp.clip(drawn, min=-limit, max=limit).astype(dtype)


def setup_inputs(seed: int = 0) -> dict:
    arg_keys = jax.random.split(jax.random.key(seed), 6)
    return {
        "amplitudes": normal_values(arg_keys[0], (N_REP, SLOTS_PART, ROWS), 1.0, 6.0, ((0, 4), (1, 64))),
        "integral_slab": normal_values(arg_keys[1], (N_REP, SLOTS_PART, IRREPS * COLS_IRREP), SLOTS ** -0.5, 0.0546875, ((0, 4), (2, 64))),
        "allowed_slots": set_ends((jax.random.randint(arg_keys[2], (IRREPS, SLOTS), 0, 8) < 7).astype(jnp.int32), jax.random.fold_in(arg_keys[2], 1), 0, 1),
        "row_energy": jnp.clip(0.5 + 2.5 * jax.random.uniform(arg_keys[3], (ROWS,), jnp.float32) ** level_of(arg_keys[3], (ROWS,), ((0, 64),), -0.2, 0.2), 0.5, 3.0),
        "col_energy": jnp.clip(0.5 + 2.5 * jax.random.uniform(arg_keys[4], (IRREPS, COLS_IRREP), jnp.float32) ** level_of(arg_keys[4], (IRREPS, COLS_IRREP), ((1, 4),), -0.2, 0.2), 0.5, 3.0),
    }


def reference(amplitudes, integral_slab, allowed_slots, row_energy, col_energy):
    irrep_blocks = []
    for irrep_index in range(IRREPS):
        amp_block = amplitudes[:, :, irrep_index * ROWS_IRREP:(irrep_index + 1) * ROWS_IRREP].reshape(SLOTS, ROWS_IRREP)
        slab_block = integral_slab[:, :, irrep_index * COLS_IRREP:(irrep_index + 1) * COLS_IRREP].reshape(SLOTS, COLS_IRREP)
        slab_block = slab_block * allowed_slots[irrep_index].astype(jnp.bfloat16)[:, None]
        cycle_term = lax.dot_general(slab_block, amp_block, (((0,), (0,)), ((), ())), preferred_element_type=jnp.float32)
        denominator = row_energy[irrep_index * ROWS_IRREP:(irrep_index + 1) * ROWS_IRREP][None, :] + col_energy[irrep_index][:, None]
        irrep_blocks.append(cycle_term / denominator)
    return jnp.concatenate(irrep_blocks, axis=1)
```

```python
import jax
import jax.numpy as jnp
from jax import lax
from jax.experimental import pallas as pl
from jax.experimental.pallas import tpu as pltpu
from jax.sharding import PartitionSpec as P

IRREPS = 8
MESH = pl.DeviceIdType.MESH

Y, Z, CORES = 4, 8, 2
ORB = Y * Z * CORES
REP = 4
LINE = 4
SLOTS_OWN = 44
PACK = 16
CHUNKS = 4
WIDE = 256
BLOCK = CHUNKS * WIDE
COLS_OWN = 128
DEEP = 3 * ORB * PACK


def transfer(src, dst, send_sem, recv_sem, orb, rep):
    return pltpu.make_async_remote_copy(
        src_ref=src,
        dst_ref=dst,
        send_sem=send_sem,
        recv_sem=recv_sem,
        device_id=(orb, rep),
        device_id_type=MESH,
    )


def settle(ref, sem):
    pltpu.make_async_copy(ref, ref, sem).wait()


def kernel(
    amp, slab_own, row_energy, col_energy, out,
    packed, arrived, slab, part, summed,
    amp_send, amp_recv, line_send, line_recv, pair_send, pair_recv, rep_send, rep_recv,
):
    me = lax.axis_index("orb")
    rep = lax.axis_index("rep")
    y, z, core = me // (Z * CORES), (me // CORES) % Z, me % CORES
    low = z % LINE
    sibling = me + 1 - 2 * core

    def target(turn):
        i, s = turn % 8, turn // 16
        odd, half = i % 2, i // 2
        dz = (1 - odd) * (half + 1) + odd * (7 - half) - 4 * (i // 7)
        dy = (s + i + 2) % Y
        dc = 1 - (turn // 8) % 2
        return (y + dy) % Y * (Z * CORES) + (z + dz) % Z * CORES + (core + dc) % CORES

    barrier = pltpu.get_barrier_semaphore()

    @pl.loop(0, ORB - 1)
    def _(turn):
        pl.semaphore_signal(barrier, inc=1, device_id=(target(turn), rep), device_id_type=MESH)

    for step in range(1, REP):
        pl.semaphore_signal(
            barrier, inc=1, device_id=(me, (rep + step) % REP), device_id_type=MESH
        )
    pl.semaphore_wait(barrier, ORB - 1 + REP - 1)

    def to_sibling(origin):
        at = origin * CORES + core
        return transfer(
            slab.at[at], slab.at[at], pair_send.at[origin], pair_recv.at[origin], sibling, rep
        )

    def up(step):
        at = jnp.maximum(low - step, 0) * CORES + core
        return transfer(
            slab.at[at], slab.at[at], line_send.at[0, step], line_recv.at[0, step],
            (me + CORES) % ORB, rep,
        )

    def down(step):
        at = jnp.minimum(low + step, LINE - 1) * CORES + core
        return transfer(
            slab.at[at], slab.at[at], line_send.at[1, step], line_recv.at[1, step],
            (me - CORES + ORB) % ORB, rep,
        )

    def send_line(step):
        @pl.when((low < LINE - 1) & (low >= step))
        def _():
            up(step).start()

        @pl.when((low > 0) & (low <= LINE - 1 - step))
        def _():
            down(step).start()

    def receive_line(step):
        @pl.when(low >= step + 1)
        def _():
            up(step).wait_recv()
            to_sibling(low - 1 - step).start()

        @pl.when(low <= LINE - 2 - step)
        def _():
            down(step).wait_recv()
            to_sibling(low + 1 + step).start()

    own = low * CORES + core
    slab[own] = slab_own[...]
    send_line(0)
    to_sibling(low).start()

    def pack(device, ref, at):
        first = pl.multiple_of(device * BLOCK, BLOCK)
        last = amp[0, 32:SLOTS_OWN, pl.ds(first + 3 * WIDE, WIDE)].astype(jnp.float32)
        for chunk in range(CHUNKS):
            columns = pl.ds(first + chunk * WIDE, WIDE)
            ref[chunk, at, :, 0:WIDE] = amp[0, 0:16, columns]
            ref[chunk, at, :, WIDE:2 * WIDE] = amp[0, 16:32, columns]
            if chunk < CHUNKS - 1:
                rest = amp[0, 32:SLOTS_OWN, columns].astype(jnp.float32)
                tail = jnp.concatenate([rest, last[4 * chunk:4 * chunk + 4]], axis=0)
                ref[chunk, at, :, 2 * WIDE:] = tail.astype(jnp.bfloat16)

    def chunk_width(chunk):
        return 3 * WIDE if chunk < CHUNKS - 1 else 2 * WIDE

    def send_block(chunk, turn):
        columns = pl.ds(0, chunk_width(chunk))
        transfer(
            packed.at[chunk, turn, :, columns], arrived.at[chunk, me, :, columns],
            amp_send.at[chunk], amp_recv.at[chunk], target(turn), rep,
        ).start()

    def send_chunk(chunk):
        @pl.loop(0, ORB - 1)
        def _(turn):
            send_block(chunk, turn)

    @pl.loop(0, ORB - 1)
    def _(turn):
        pack(target(turn), packed, turn)
        send_block(0, turn)

    pack(me, arrived, me)
    receive_line(0)
    send_line(1)
    send_chunk(1)
    receive_line(1)
    send_line(2)
    send_chunk(2)
    receive_line(2)
    send_chunk(3)

    for origin in range(LINE):
        settle(slab.at[origin], pair_recv.at[origin])

    def contract(chunk):
        @pl.loop(0, REP)
        def _(step):
            block = (rep + 1 + step) % REP
            total = jnp.zeros((WIDE, WIDE), jnp.float32)
            for third in range(3):
                rows = slab[pl.ds(block * 2, 2), :, third * 1024:(third + 1) * 1024]
                held = arrived[chunk, :, :, third * WIDE:(third + 1) * WIDE]
                total += jnp.dot(
                    rows.reshape(2 * COLS_OWN, 1024),
                    held.reshape(1024, WIDE),
                    preferred_element_type=jnp.float32,
                )
            part[chunk, step] = total

            @pl.when(step < REP - 1)
            def _():
                transfer(
                    part.at[chunk, step], summed.at[chunk, step],
                    rep_send.at[chunk], rep_recv.at[chunk], me, block,
                ).start()

    def finish(chunk):
        settle(summed.at[chunk], rep_recv.at[chunk])
        columns = slice(chunk * WIDE, (chunk + 1) * WIDE)
        total = part[chunk, REP - 1] + summed[chunk, 0] + summed[chunk, 1] + summed[chunk, 2]
        out[:, columns] = total / (col_energy[...] + row_energy[:, columns])

    def receive_chunk(chunk):
        settle(
            arrived.at[chunk, pl.ds(0, ORB - 1), :, pl.ds(0, chunk_width(chunk))],
            amp_recv.at[chunk],
        )

    for chunk in range(CHUNKS - 1):
        receive_chunk(chunk)
        contract(chunk)
        if chunk > 0:
            finish(chunk - 1)

    low_rows = lax.broadcasted_iota(jnp.int32, (ORB * PACK, WIDE), 0) % PACK
    tails = [
        arrived[chunk, :, :, 2 * WIDE:].reshape(ORB * PACK, WIDE).astype(jnp.float32)
        for chunk in range(3)
    ]
    tail = jnp.where(
        low_rows < 4,
        pltpu.roll(tails[0], ORB * PACK - 12, 0),
        jnp.where(
            low_rows < 8,
            pltpu.roll(tails[1], ORB * PACK - 8, 0),
            pltpu.roll(tails[2], ORB * PACK - 4, 0),
        ),
    )
    arrived[CHUNKS - 1, :, :, 2 * WIDE:] = tail.astype(jnp.bfloat16).reshape(ORB, PACK, WIDE)
    finish(CHUNKS - 2)
    receive_chunk(CHUNKS - 1)
    contract(CHUNKS - 1)
    finish(CHUNKS - 1)

    for chunk in range(CHUNKS):
        settle(
            packed.at[chunk, pl.ds(0, ORB - 1), :, pl.ds(0, chunk_width(chunk))],
            amp_send.at[chunk],
        )
        settle(part.at[chunk, pl.ds(0, REP - 1)], rep_send.at[chunk])
    for step in range(LINE - 1):

        @pl.when((low < LINE - 1) & (low >= step))
        def _():
            up(step).wait_send()

        @pl.when((low > 0) & (low <= LINE - 1 - step))
        def _():
            down(step).wait_send()

    for origin in range(LINE):
        to_sibling(origin).wait_send()


def exchange(amplitudes, slab_own, row_energy, col_energy):
    vmem = pl.BlockSpec(memory_space=pltpu.VMEM)
    return pl.pallas_call(
        kernel,
        out_shape=jax.ShapeDtypeStruct((COLS_OWN * 2, BLOCK), jnp.float32),
        in_specs=[vmem] * 4,
        out_specs=vmem,
        scratch_shapes=[
            pltpu.VMEM((CHUNKS, ORB, PACK, 3 * WIDE), jnp.bfloat16),
            pltpu.VMEM((CHUNKS, ORB, PACK, 3 * WIDE), jnp.bfloat16),
            pltpu.VMEM((LINE * CORES, COLS_OWN, DEEP), jnp.bfloat16),
            pltpu.VMEM((CHUNKS, REP, WIDE, WIDE), jnp.float32),
            pltpu.VMEM((CHUNKS, REP - 1, WIDE, WIDE), jnp.float32),
            pltpu.SemaphoreType.DMA((CHUNKS,)),
            pltpu.SemaphoreType.DMA((CHUNKS,)),
            pltpu.SemaphoreType.DMA((2, LINE - 1)),
            pltpu.SemaphoreType.DMA((2, LINE - 1)),
            pltpu.SemaphoreType.DMA((LINE,)),
            pltpu.SemaphoreType.DMA((LINE,)),
            pltpu.SemaphoreType.DMA((CHUNKS,)),
            pltpu.SemaphoreType.DMA((CHUNKS,)),
        ],
        compiler_params=pltpu.CompilerParams(
            collective_id=0, has_side_effects=True, vmem_limit_bytes=56 * 2**20
        ),
        cost_estimate=pl.CostEstimate(
            flops=2 * 1024 * BLOCK * DEEP, bytes_accessed=8 * 2**20, transcendentals=0
        ),
    )(amplitudes, slab_own, row_energy, col_energy)


def per_device(amplitudes, integral_slab, allowed_slots, row_energy, col_energy):
    irrep_index = lax.axis_index("orb") // (lax.axis_size("orb") // IRREPS)
    allowed_row = lax.dynamic_slice_in_dim(allowed_slots, irrep_index, 1, 0)[0]
    live = integral_slab[0] * allowed_row.astype(jnp.bfloat16)[:, None]
    live = jnp.pad(live.reshape(ORB, SLOTS_OWN, COLS_OWN), ((0, 0), (0, 48 - SLOTS_OWN), (0, 0)))
    live = live.reshape(ORB, 3, PACK, COLS_OWN).transpose(3, 1, 0, 2).reshape(COLS_OWN, DEEP)
    col_row = lax.dynamic_slice_in_dim(col_energy, irrep_index, 1, 0)[0]
    return exchange(amplitudes, live, row_energy[None, :], col_row[:, None])


def solution(mesh):
    placed = (
        P("rep", "orb", None),
        P("rep", None, "orb"),
        P(None, "rep"),
        P("orb"),
        P(None, "rep"),
    )
    return jax.shard_map(
        per_device, mesh=mesh, in_specs=placed, out_specs=P("rep", "orb"), check_vma=False
    )
```

```python
import jax
import jax.numpy as jnp
from jax import lax
from jax.experimental import pallas as pl
from jax.experimental.pallas import tpu as pltpu
from jax.sharding import PartitionSpec as P

IRREPS = 8
MESH = pl.DeviceIdType.MESH

Y, Z, CORES = 4, 8, 2
ORB = Y * Z * CORES
REP = 4
LINE = 4
QUARTERS = 4
SOURCES = ORB // QUARTERS
TARGETS = ORB // 2
SLOTS_OWN = 44
PACK = 16
THIRDS = 3
CHUNKS = 8
FULL = 6
NARROW = 128
WIDE = 2 * NARROW
BLOCK = CHUNKS * NARROW
COLS_OWN = 128
COLS_OUT = 256
QUARTER = THIRDS * SOURCES * PACK
DEEP = 2 * QUARTER
ROWS_Y = Z * CORES * SLOTS_OWN
COLUMNS = Z * CORES * THIRDS * PACK
PIECES = [(chunk, pl.ds(0, WIDE)) for chunk in range(CHUNKS - 1)]
PIECES += [(CHUNKS - 1, pl.ds(0, NARROW)), (CHUNKS - 1, pl.ds(NARROW, NARROW))]


def transfer(src, dst, send_sem, recv_sem, orb, rep):
    return pltpu.make_async_remote_copy(
        src_ref=src,
        dst_ref=dst,
        send_sem=send_sem,
        recv_sem=recv_sem,
        device_id=(orb, rep),
        device_id_type=MESH,
    )


def settle(ref, sem):
    pltpu.make_async_copy(ref, ref, sem).wait()


def kernel(
    amp, integrals, allowed, row_energy, col_energy, out,
    stage, packed, arrived, order, slab_own, slab, part, summed, both, cross,
    stage_sem, amp_send, amp_recv, line_send, line_recv, pair_send, pair_recv,
    rep_send, rep_recv, cross_send, cross_recv,
):
    me = lax.axis_index("orb")
    rep = lax.axis_index("rep")
    y, z, core = me // (Z * CORES), (me // CORES) % Z, me % CORES
    low, high = z % LINE, z // LINE
    upper = low // 2
    sibling = me + 1 - 2 * core
    partner = me + 2 * CORES - 4 * CORES * upper

    def device(y, z, core):
        return y * (Z * CORES) + z * CORES + core

    def target(turn):
        kind, s = turn % 4, turn // 4
        near = kind % 2
        half = (1 - near) * (kind // 2) + near * (upper + (kind // 2) * (1 - 2 * upper))
        group = (high + 1 - near) % 2
        quarter = ((z - LINE * group + Z + 3) // 2) % QUARTERS
        place = (quarter - half + LINE) % LINE
        to_y = (y + s + kind + 2) % Y
        to_core = (core + 1 - s // 4) % CORES
        return to_y, group, place, to_core, half

    def target_id(turn):
        to_y, group, place, to_core, _ = target(turn)
        return device(to_y, group * LINE + place, to_core)

    def first_rows(turn):
        to_y, group, place, to_core, _ = target(turn)
        return device(to_y, group * LINE + place % 2, to_core)

    def load(turn, side):
        base = pl.multiple_of((first_rows(turn) + side * 2 * CORES) * BLOCK, BLOCK)
        return pltpu.make_async_copy(
            amp.at[0, :, pl.ds(base, BLOCK)], stage.at[turn, side], stage_sem.at[turn, side]
        )

    @pl.loop(0, TARGETS)
    def _(turn):
        load(turn, 0).start()
        load(turn, 1).start()

    barrier = pltpu.get_barrier_semaphore()

    @pl.loop(0, TARGETS)
    def _(index):
        step = index // (Y * CORES)
        from_z = (LINE * high + 2 * low - 3 + step + Z) % Z
        source = device((index // CORES) % Y, from_z, index % CORES)

        @pl.when(source != me)
        def _():
            pl.semaphore_signal(barrier, inc=1, device_id=(source, rep), device_id_type=MESH)

    for step in range(1, REP):
        pl.semaphore_signal(
            barrier, inc=1, device_id=(me, (rep + step) % REP), device_id_type=MESH
        )
    for step in range(1, LINE):
        pl.semaphore_signal(
            barrier, inc=1,
            device_id=(me + CORES * ((low + step) % LINE - low), rep), device_id_type=MESH,
        )
    pl.semaphore_signal(barrier, inc=1, device_id=(sibling, rep), device_id_type=MESH)
    pl.semaphore_wait(barrier, TARGETS - 1 + REP - 1 + LINE - 1 + 1)

    own = low * CORES + core

    def quarter_of(place, half):
        quarter = (place + half + 2 + 2 * high) % QUARTERS
        return pl.ds(pl.multiple_of(quarter * QUARTER, QUARTER), QUARTER)

    def order_slab():
        across = lax.broadcasted_iota(jnp.int32, (1, COLUMNS), 1)
        piece, within = across // 64, across % 64
        slot = piece % THIRDS * PACK + within % PACK
        from_z = (2 * (piece // THIRDS) + 1 + within // 32) % Z
        row = (from_z * CORES + within // PACK % CORES) * SLOTS_OWN + slot
        row = jnp.where(slot < SLOTS_OWN, row, -1)
        down = lax.broadcasted_iota(jnp.int32, (ROWS_Y, COLUMNS), 0)
        order[...] = jnp.where(down == row, 1.0, 0.0).astype(jnp.bfloat16)
        irrep = lax.broadcasted_iota(jnp.int32, (IRREPS, COLUMNS), 0)
        for at_y in range(Y):
            rows = slice(at_y * ROWS_Y, (at_y + 1) * ROWS_Y)
            live = lax.dot_general(
                integrals[0, rows], order[...], (((0,), (0,)), ((), ())),
                preferred_element_type=jnp.float32,
            )
            mask = jnp.dot(
                allowed[:, rows].astype(jnp.float32).astype(jnp.bfloat16), order[...],
                preferred_element_type=jnp.float32,
            )
            mask = jnp.sum(
                jnp.where(irrep == me // (ORB // IRREPS), mask, 0.0), axis=0, keepdims=True
            )
            live = (live * mask).astype(jnp.bfloat16)
            for piece in range(QUARTERS * THIRDS):
                first = piece * SOURCES * PACK + at_y * 64
                slab_own[:, first:first + 64] = live[:, piece * 64:(piece + 1) * 64]

    def to_sibling(step):
        at = (low - step + LINE) % LINE * CORES + core
        return transfer(
            slab.at[at], slab.at[at], pair_send.at[step], pair_recv.at[step], sibling, rep
        )

    def send_slab(step, half):
        place = (low + step) % LINE
        transfer(
            slab_own.at[:, quarter_of(place, half)],
            slab.at[own, :, pl.ds(half * QUARTER, QUARTER)],
            line_send.at[step - 1], line_recv.at[step - 1], me + CORES * (place - low), rep,
        ).start()

    def pack(turn, store):
        for side in range(2):
            load(turn, side).wait()
            lanes = slice(side * NARROW, (side + 1) * NARROW)

            def read(first, last, chunk):
                return stage[turn, side, first:last, chunk * NARROW:(chunk + 1) * NARROW]

            lasts = [read(32, SLOTS_OWN, chunk).astype(jnp.float32) for chunk in range(FULL, CHUNKS)]
            for chunk in range(CHUNKS):
                store(chunk, 0, lanes, read(0, 16, chunk))
                store(chunk, 1, lanes, read(16, 32, chunk))
                if chunk < FULL:
                    rest = read(32, SLOTS_OWN, chunk).astype(jnp.float32)
                    at = 4 * (chunk % 3)
                    tail = jnp.concatenate([rest, lasts[chunk // 3][at:at + 4]], axis=0)
                    store(chunk, 2, lanes, tail.astype(jnp.bfloat16))

    source_at = y * (2 * CORES) + (z + 1) % 2 * CORES + core

    def thirds(chunk):
        return pl.ds(0, THIRDS if chunk < FULL else 2)

    def send_block(piece, turn):
        chunk, lanes = PIECES[piece]
        half = target(turn)[-1]
        transfer(
            packed.at[chunk, turn, thirds(chunk), :, lanes],
            arrived.at[chunk, half, thirds(chunk), source_at, :, lanes],
            amp_send.at[piece], amp_recv.at[piece], target_id(turn), rep,
        ).start()

    def send_piece(piece, first=0, last=TARGETS - 1):
        @pl.loop(first, last)
        def _(turn):
            send_block(piece, turn)

    def sent(piece):
        chunk, lanes = PIECES[piece]
        return packed.at[chunk, pl.ds(0, TARGETS - 1), thirds(chunk), :, lanes]

    @pl.loop(0, TARGETS - 1)
    def _(turn):
        def store(chunk, third, lanes, value):
            packed[chunk, turn, third, :, lanes] = value

        pack(turn, store)
        send_block(0, turn)

    def store_own(chunk, third, lanes, value):
        arrived[chunk, 1 - upper, third, source_at, :, lanes] = value

    pack(TARGETS - 1, store_own)
    order_slab()
    for part_of in range(6):
        send_slab(1 + part_of % 3, part_of // 3)
        send_piece(1, part_of * 5, part_of * 5 + 5 if part_of < 5 else TARGETS - 1)
    for half in range(2):
        slab[own, :, half * QUARTER:(half + 1) * QUARTER] = slab_own[:, quarter_of(low, half)]
    to_sibling(0).start()
    send_piece(2)
    for step in range(1, LINE):
        at = (low - step + LINE) % LINE * CORES + core
        settle(slab.at[at], line_recv.at[step - 1])
        to_sibling(step).start()
    send_piece(3)
    for step in range(LINE):
        settle(slab.at[own], pair_recv.at[step])

    def contract(piece):
        chunk, lanes = PIECES[piece]

        @pl.loop(0, REP)
        def _(step):
            block = (rep + 1 + step) % REP
            rows = slab[pl.ds(block * 2, 2)].reshape(COLS_OUT, DEEP)
            part[chunk, step, :, lanes] = jnp.dot(
                rows,
                arrived[chunk, :, :, :, :, lanes].reshape(DEEP, lanes.size),
                preferred_element_type=jnp.float32,
            )

            @pl.when(step < REP - 1)
            def _():
                transfer(
                    part.at[chunk, step, :, lanes], summed.at[chunk, step, :, lanes],
                    rep_send.at[piece], rep_recv.at[piece], me, block,
                ).start()

    own_lanes = pl.ds(pl.multiple_of(upper * NARROW, NARROW), NARROW)
    other_lanes = pl.ds(pl.multiple_of((1 - upper) * NARROW, NARROW), NARROW)

    def to_partner(chunk):
        return transfer(
            both.at[chunk, :, other_lanes], cross.at[chunk],
            cross_send.at[chunk], cross_recv.at[chunk], partner, rep,
        )

    def sum_quarters(piece):
        chunk, lanes = PIECES[piece]
        settle(summed.at[chunk, :, :, lanes], rep_recv.at[piece])
        total = part[chunk, REP - 1, :, lanes]
        for step in range(REP - 1):
            total += summed[chunk, step, :, lanes]
        both[chunk, :, lanes] = total
        if lanes.size == WIDE:
            to_partner(chunk).start()
        else:

            @pl.when(upper == 1 - lanes.start // NARROW)
            def _():
                to_partner(chunk).start()

    def finish(chunk):
        to_partner(chunk).wait_recv()
        columns = slice(chunk * NARROW, (chunk + 1) * NARROW)
        total = both[chunk, :, own_lanes] + cross[chunk]
        out[:, columns] = total / (col_energy[...] + row_energy[:, columns])

    def gather_tail(chunk):
        rows = 2 * SOURCES * PACK
        place = lax.broadcasted_iota(jnp.int32, (rows, WIDE), 0) % PACK
        first = (chunk - FULL) * 3
        tails = [
            pltpu.roll(
                arrived[first + i, :, 2].reshape(rows, WIDE).astype(jnp.float32),
                rows - 12 + 4 * i,
                0,
            )
            for i in range(3)
        ]
        tail = jnp.where(place < 4, tails[0], jnp.where(place < 8, tails[1], tails[2]))
        arrived[chunk, :, 2] = tail.astype(jnp.bfloat16).reshape(2, SOURCES, PACK, WIDE)

    for piece, (chunk, _) in enumerate(PIECES):
        settle(sent(piece), amp_recv.at[piece])
        if piece + 4 < len(PIECES):
            send_piece(piece + 4)
        contract(piece)
        if piece >= 1:
            sum_quarters(piece - 1)
        if 2 <= piece <= CHUNKS:
            finish(piece - 2)
        if piece == 2:
            gather_tail(FULL)
        if piece == 5:
            gather_tail(FULL + 1)
    sum_quarters(len(PIECES) - 1)
    finish(CHUNKS - 1)

    for piece, (chunk, lanes) in enumerate(PIECES):
        settle(sent(piece), amp_send.at[piece])
        settle(part.at[chunk, pl.ds(0, REP - 1), :, lanes], rep_send.at[piece])
    for chunk in range(CHUNKS):
        to_partner(chunk).wait_send()
    for step in range(LINE - 1):
        settle(slab.at[own], line_send.at[step])
    for step in range(LINE):
        settle(slab.at[own], pair_send.at[step])


def per_device(amplitudes, integral_slab, allowed_slots, row_energy, col_energy):
    irrep_index = lax.axis_index("orb") // (lax.axis_size("orb") // IRREPS)
    col_row = lax.dynamic_slice_in_dim(col_energy, irrep_index, 1, 0)[0]
    vmem = pl.BlockSpec(memory_space=pltpu.VMEM)
    pairs = lambda count: [pltpu.SemaphoreType.DMA((count,))] * 2
    return pl.pallas_call(
        kernel,
        out_shape=jax.ShapeDtypeStruct((COLS_OUT, BLOCK), jnp.float32),
        in_specs=[pl.BlockSpec(memory_space=pl.ANY)] + [vmem] * 4,
        out_specs=vmem,
        scratch_shapes=[
            pltpu.VMEM((TARGETS, 2, SLOTS_OWN, BLOCK), jnp.bfloat16),
            pltpu.VMEM((CHUNKS, TARGETS, THIRDS, PACK, WIDE), jnp.bfloat16),
            pltpu.VMEM((CHUNKS, 2, THIRDS, SOURCES, PACK, WIDE), jnp.bfloat16),
            pltpu.VMEM((ROWS_Y, COLUMNS), jnp.bfloat16),
            pltpu.VMEM((COLS_OWN, QUARTERS * QUARTER), jnp.bfloat16),
            pltpu.VMEM((LINE * CORES, COLS_OWN, DEEP), jnp.bfloat16),
            pltpu.VMEM((CHUNKS, REP, COLS_OUT, WIDE), jnp.float32),
            pltpu.VMEM((CHUNKS, REP - 1, COLS_OUT, WIDE), jnp.float32),
            pltpu.VMEM((CHUNKS, COLS_OUT, WIDE), jnp.float32),
            pltpu.VMEM((CHUNKS, COLS_OUT, NARROW), jnp.float32),
            pltpu.SemaphoreType.DMA((TARGETS, 2)),
            *pairs(len(PIECES)),
            *pairs(LINE - 1),
            *pairs(LINE),
            *pairs(len(PIECES)),
            *pairs(CHUNKS),
        ],
        compiler_params=pltpu.CompilerParams(
            collective_id=0, has_side_effects=True, vmem_limit_bytes=56 * 2**20
        ),
        cost_estimate=pl.CostEstimate(
            flops=2 * 1024 * WIDE * CHUNKS * DEEP, bytes_accessed=8 * 2**20, transcendentals=0
        ),
    )(amplitudes, integral_slab, allowed_slots, row_energy[None, :], col_row[:, None])


def solution(mesh):
    placed = (
        P("rep", "orb", None),
        P("rep", None, "orb"),
        P(None, "rep"),
        P("orb"),
        P(None, "rep"),
    )
    return jax.shard_map(
        per_device, mesh=mesh, in_specs=placed, out_specs=P("rep", "orb"), check_vma=False
    )
```

```python
import jax
import jax.numpy as jnp
from jax import lax
from jax.experimental import pallas as pl
from jax.experimental.pallas import tpu as pltpu
from jax.sharding import PartitionSpec as P

IRREPS = 8
MESH = pl.DeviceIdType.MESH

Y, Z, CORES = 4, 8, 2
ORB = Y * Z * CORES
REP = 4
LINE = 4
QUARTERS = 4
SOURCES = ORB // QUARTERS
TARGETS = ORB // 2
SLOTS_OWN = 44
PACK = 16
THIRDS = 3
CHUNKS = 8
FULL = 6
NARROW = 128
WIDE = 2 * NARROW
BLOCK = CHUNKS * NARROW
COLS_OWN = 128
COLS_OUT = 256
HALF = COLS_OUT // 2
OPPOSITE, OWN, BESIDE = 0, 2, (1, 3)
QUARTER = THIRDS * SOURCES * PACK
DEEP = 2 * QUARTER
ROWS_Y = Z * CORES * SLOTS_OWN
COLUMNS = Z * CORES * THIRDS * PACK
PIECES = [(chunk, pl.ds(0, WIDE)) for chunk in range(CHUNKS - 1)]
PIECES += [(CHUNKS - 1, pl.ds(0, NARROW)), (CHUNKS - 1, pl.ds(NARROW, NARROW))]


def transfer(src, dst, send_sem, recv_sem, orb, rep):
    return pltpu.make_async_remote_copy(
        src_ref=src,
        dst_ref=dst,
        send_sem=send_sem,
        recv_sem=recv_sem,
        device_id=(orb, rep),
        device_id_type=MESH,
    )


def settle(ref, sem):
    pltpu.make_async_copy(ref, ref, sem).wait()


def kernel(
    amp, integrals, allowed, row_energy, col_energy, out,
    stage, packed, arrived, order, slab_own, slab, part, near, summed, both, cross,
    stage_sem, amp_send, amp_recv, line_send, line_recv, pair_send, pair_recv,
    near_recv, rep_send, rep_recv, cross_send, cross_recv,
):
    me = lax.axis_index("orb")
    rep = lax.axis_index("rep")
    y, z, core = me // (Z * CORES), (me // CORES) % Z, me % CORES
    low, high = z % LINE, z // LINE
    upper = low // 2
    sibling = me + 1 - 2 * core
    partner = me + 2 * CORES - 4 * CORES * upper

    def device(y, z, core):
        return y * (Z * CORES) + z * CORES + core

    def target(turn):
        kind, s = turn % 4, turn // 4
        near = kind % 2
        half = (1 - near) * (kind // 2) + near * (upper + (kind // 2) * (1 - 2 * upper))
        group = (high + 1 - near) % 2
        quarter = ((z - LINE * group + Z + 3) // 2) % QUARTERS
        place = (quarter - half + LINE) % LINE
        to_y = (y + s + kind + 2) % Y
        to_core = (core + 1 - s // 4) % CORES
        return to_y, group, place, to_core, half

    def target_id(turn):
        to_y, group, place, to_core, _ = target(turn)
        return device(to_y, group * LINE + place, to_core)

    def first_rows(turn):
        to_y, group, place, to_core, _ = target(turn)
        return device(to_y, group * LINE + place % 2, to_core)

    def load(turn, side):
        base = pl.multiple_of((first_rows(turn) + side * 2 * CORES) * BLOCK, BLOCK)
        return pltpu.make_async_copy(
            amp.at[0, :, pl.ds(base, BLOCK)], stage.at[turn, side], stage_sem.at[turn, side]
        )

    @pl.loop(0, TARGETS)
    def _(turn):
        load(turn, 0).start()
        load(turn, 1).start()

    barrier = pltpu.get_barrier_semaphore()

    @pl.loop(0, TARGETS)
    def _(index):
        step = index // (Y * CORES)
        from_z = (LINE * high + 2 * low - 3 + step + Z) % Z
        source = device((index // CORES) % Y, from_z, index % CORES)

        @pl.when(source != me)
        def _():
            pl.semaphore_signal(barrier, inc=1, device_id=(source, rep), device_id_type=MESH)

    for step in range(1, REP):
        pl.semaphore_signal(
            barrier, inc=1, device_id=(me, (rep + step) % REP), device_id_type=MESH
        )
    for step in range(1, LINE):
        pl.semaphore_signal(
            barrier, inc=1,
            device_id=(me + CORES * ((low + step) % LINE - low), rep), device_id_type=MESH,
        )
    pl.semaphore_signal(barrier, inc=1, device_id=(sibling, rep), device_id_type=MESH)
    pl.semaphore_wait(barrier, TARGETS - 1 + REP - 1 + LINE - 1 + 1)

    own = low * CORES + core

    def quarter_of(place, half):
        quarter = (place + half + 2 + 2 * high) % QUARTERS
        return pl.ds(pl.multiple_of(quarter * QUARTER, QUARTER), QUARTER)

    def order_slab():
        across = lax.broadcasted_iota(jnp.int32, (1, COLUMNS), 1)
        piece, within = across // 64, across % 64
        slot = piece % THIRDS * PACK + within % PACK
        from_z = (2 * (piece // THIRDS) + 1 + within // 32) % Z
        row = (from_z * CORES + within // PACK % CORES) * SLOTS_OWN + slot
        row = jnp.where(slot < SLOTS_OWN, row, -1)
        down = lax.broadcasted_iota(jnp.int32, (ROWS_Y, COLUMNS), 0)
        order[...] = jnp.where(down == row, 1.0, 0.0).astype(jnp.bfloat16)
        irrep = lax.broadcasted_iota(jnp.int32, (IRREPS, COLUMNS), 0)
        for at_y in range(Y):
            rows = slice(at_y * ROWS_Y, (at_y + 1) * ROWS_Y)
            live = lax.dot_general(
                integrals[0, rows], order[...], (((0,), (0,)), ((), ())),
                preferred_element_type=jnp.float32,
            )
            mask = jnp.dot(
                allowed[:, rows].astype(jnp.float32).astype(jnp.bfloat16), order[...],
                preferred_element_type=jnp.float32,
            )
            mask = jnp.sum(
                jnp.where(irrep == me // (ORB // IRREPS), mask, 0.0), axis=0, keepdims=True
            )
            live = (live * mask).astype(jnp.bfloat16)
            for piece in range(QUARTERS * THIRDS):
                first = piece * SOURCES * PACK + at_y * 64
                slab_own[:, first:first + 64] = live[:, piece * 64:(piece + 1) * 64]

    def to_sibling(step):
        at = (low - step + LINE) % LINE * CORES + core
        return transfer(
            slab.at[at], slab.at[at], pair_send.at[step], pair_recv.at[step], sibling, rep
        )

    def send_slab(step, half):
        place = (low + step) % LINE
        transfer(
            slab_own.at[:, quarter_of(place, half)],
            slab.at[own, :, pl.ds(half * QUARTER, QUARTER)],
            line_send.at[step - 1], line_recv.at[step - 1], me + CORES * (place - low), rep,
        ).start()

    def pack(turn, store):
        for side in range(2):
            load(turn, side).wait()
            lanes = slice(side * NARROW, (side + 1) * NARROW)

            def read(first, last, chunk):
                return stage[turn, side, first:last, chunk * NARROW:(chunk + 1) * NARROW]

            lasts = [read(32, SLOTS_OWN, chunk).astype(jnp.float32) for chunk in range(FULL, CHUNKS)]
            for chunk in range(CHUNKS):
                store(chunk, 0, lanes, read(0, 16, chunk))
                store(chunk, 1, lanes, read(16, 32, chunk))
                if chunk < FULL:
                    rest = read(32, SLOTS_OWN, chunk).astype(jnp.float32)
                    at = 4 * (chunk % 3)
                    tail = jnp.concatenate([rest, lasts[chunk // 3][at:at + 4]], axis=0)
                    store(chunk, 2, lanes, tail.astype(jnp.bfloat16))

    source_at = y * (2 * CORES) + (z + 1) % 2 * CORES + core

    def thirds(chunk):
        return pl.ds(0, THIRDS if chunk < FULL else 2)

    def send_block(piece, turn):
        chunk, lanes = PIECES[piece]
        half = target(turn)[-1]
        transfer(
            packed.at[chunk, turn, thirds(chunk), :, lanes],
            arrived.at[chunk, half, thirds(chunk), source_at, :, lanes],
            amp_send.at[piece], amp_recv.at[piece], target_id(turn), rep,
        ).start()

    def send_piece(piece, first=0, last=TARGETS - 1):
        @pl.loop(first, last)
        def _(turn):
            send_block(piece, turn)

    def sent(piece):
        chunk, lanes = PIECES[piece]
        return packed.at[chunk, pl.ds(0, TARGETS - 1), thirds(chunk), :, lanes]

    @pl.loop(0, TARGETS - 1)
    def _(turn):
        def store(chunk, third, lanes, value):
            packed[chunk, turn, third, :, lanes] = value

        pack(turn, store)
        send_block(0, turn)

    def store_own(chunk, third, lanes, value):
        arrived[chunk, 1 - upper, third, source_at, :, lanes] = value

    pack(TARGETS - 1, store_own)
    order_slab()
    for part_of in range(6):
        send_slab(1 + part_of % 3, part_of // 3)
        send_piece(1, part_of * 5, part_of * 5 + 5 if part_of < 5 else TARGETS - 1)
    for half in range(2):
        slab[own, :, half * QUARTER:(half + 1) * QUARTER] = slab_own[:, quarter_of(low, half)]
    to_sibling(0).start()
    send_piece(2)
    for step in range(1, LINE):
        at = (low - step + LINE) % LINE * CORES + core
        settle(slab.at[at], line_recv.at[step - 1])
        to_sibling(step).start()
    for step in range(LINE):
        settle(slab.at[own], pair_recv.at[step])

    def to_side(piece, way, src, dst, sem):
        return transfer(
            src, dst, rep_send.at[piece], sem, me, (rep + 1 + 2 * way) % REP
        )

    def half_rows(way):
        return pl.ds(way * HALF, HALF)

    def through(piece, way):
        chunk, lanes = PIECES[piece]
        return to_side(
            piece, way, part.at[chunk, OPPOSITE, half_rows(way), lanes],
            near.at[chunk, way, :, lanes], near_recv.at[piece],
        )

    def direct(piece, way, half):
        chunk, lanes = PIECES[piece]
        rows = half_rows(half)
        return to_side(
            piece, way, part.at[chunk, BESIDE[way], rows, lanes],
            summed.at[chunk, way, rows, lanes], rep_recv.at[piece],
        )

    def contract(piece):
        chunk, lanes = PIECES[piece]

        @pl.loop(0, REP)
        def _(step):
            block = (rep + 2 + 3 * step) % REP
            rows = slab[pl.ds(block * 2, 2)].reshape(COLS_OUT, DEEP)
            part[chunk, step, :, lanes] = jnp.dot(
                rows,
                arrived[chunk, :, :, :, :, lanes].reshape(DEEP, lanes.size),
                preferred_element_type=jnp.float32,
            )

            @pl.when(step == OPPOSITE)
            def _():
                through(piece, 0).start()
                through(piece, 1).start()

            for way in range(2):

                @pl.when(step == BESIDE[way])
                def _():
                    direct(piece, way, 1 - way).start()

    def pass_on(piece):
        chunk, lanes = PIECES[piece]
        settle(near.at[chunk, :, :, lanes], near_recv.at[piece])
        for way in range(2):
            part[chunk, BESIDE[way], half_rows(way), lanes] += near[chunk, way, :, lanes]
            direct(piece, way, way).start()

    own_lanes = pl.ds(pl.multiple_of(upper * NARROW, NARROW), NARROW)
    other_lanes = pl.ds(pl.multiple_of((1 - upper) * NARROW, NARROW), NARROW)

    def to_partner(chunk):
        return transfer(
            both.at[chunk, :, other_lanes], cross.at[chunk],
            cross_send.at[chunk], cross_recv.at[chunk], partner, rep,
        )

    def sum_quarters(piece):
        chunk, lanes = PIECES[piece]
        settle(summed.at[chunk, :, :, lanes], rep_recv.at[piece])
        total = part[chunk, OWN, :, lanes] + summed[chunk, 0, :, lanes]
        both[chunk, :, lanes] = total + summed[chunk, 1, :, lanes]
        if lanes.size == WIDE:
            to_partner(chunk).start()
        else:

            @pl.when(upper == 1 - lanes.start // NARROW)
            def _():
                to_partner(chunk).start()

    def finish(chunk):
        to_partner(chunk).wait_recv()
        columns = slice(chunk * NARROW, (chunk + 1) * NARROW)
        total = both[chunk, :, own_lanes] + cross[chunk]
        out[:, columns] = total / (col_energy[...] + row_energy[:, columns])

    def gather_tail(chunk):
        rows = 2 * SOURCES * PACK
        place = lax.broadcasted_iota(jnp.int32, (rows, WIDE), 0) % PACK
        first = (chunk - FULL) * 3
        tails = [
            pltpu.roll(
                arrived[first + i, :, 2].reshape(rows, WIDE).astype(jnp.float32),
                rows - 12 + 4 * i,
                0,
            )
            for i in range(3)
        ]
        tail = jnp.where(place < 4, tails[0], jnp.where(place < 8, tails[1], tails[2]))
        arrived[chunk, :, 2] = tail.astype(jnp.bfloat16).reshape(2, SOURCES, PACK, WIDE)

    for piece, (chunk, _) in enumerate(PIECES):
        settle(sent(piece), amp_recv.at[piece])
        if piece + 3 < len(PIECES):
            send_piece(piece + 3)
        contract(piece)
        if piece >= 1:
            sum_quarters(piece - 1)
        if 2 <= piece <= CHUNKS:
            finish(piece - 2)
        if piece == 2:
            gather_tail(FULL)
        if piece == 5:
            gather_tail(FULL + 1)
        pass_on(piece)
    sum_quarters(len(PIECES) - 1)
    finish(CHUNKS - 1)

    for piece, (chunk, lanes) in enumerate(PIECES):
        settle(sent(piece), amp_send.at[piece])
        settle(part.at[chunk, pl.ds(0, REP - 1), :, lanes], rep_send.at[piece])
    for chunk in range(CHUNKS):
        to_partner(chunk).wait_send()
    for step in range(LINE - 1):
        settle(slab.at[own], line_send.at[step])
    for step in range(LINE):
        settle(slab.at[own], pair_send.at[step])


def per_device(amplitudes, integral_slab, allowed_slots, row_energy, col_energy):
    irrep_index = lax.axis_index("orb") // (lax.axis_size("orb") // IRREPS)
    col_row = lax.dynamic_slice_in_dim(col_energy, irrep_index, 1, 0)[0]
    vmem = pl.BlockSpec(memory_space=pltpu.VMEM)
    pairs = lambda count: [pltpu.SemaphoreType.DMA((count,))] * 2
    return pl.pallas_call(
        kernel,
        out_shape=jax.ShapeDtypeStruct((COLS_OUT, BLOCK), jnp.float32),
        in_specs=[pl.BlockSpec(memory_space=pl.ANY)] + [vmem] * 4,
        out_specs=vmem,
        scratch_shapes=[
            pltpu.VMEM((TARGETS, 2, SLOTS_OWN, BLOCK), jnp.bfloat16),
            pltpu.VMEM((CHUNKS, TARGETS, THIRDS, PACK, WIDE), jnp.bfloat16),
            pltpu.VMEM((CHUNKS, 2, THIRDS, SOURCES, PACK, WIDE), jnp.bfloat16),
            pltpu.VMEM((ROWS_Y, COLUMNS), jnp.bfloat16),
            pltpu.VMEM((COLS_OWN, QUARTERS * QUARTER), jnp.bfloat16),
            pltpu.VMEM((LINE * CORES, COLS_OWN, DEEP), jnp.bfloat16),
            pltpu.VMEM((CHUNKS, REP, COLS_OUT, WIDE), jnp.float32),
            pltpu.VMEM((CHUNKS, 2, HALF, WIDE), jnp.float32),
            pltpu.VMEM((CHUNKS, 2, COLS_OUT, WIDE), jnp.float32),
            pltpu.VMEM((CHUNKS, COLS_OUT, WIDE), jnp.float32),
            pltpu.VMEM((CHUNKS, COLS_OUT, NARROW), jnp.float32),
            pltpu.SemaphoreType.DMA((TARGETS, 2)),
            *pairs(len(PIECES)),
            *pairs(LINE - 1),
            *pairs(LINE),
            pltpu.SemaphoreType.DMA((len(PIECES),)),
            *pairs(len(PIECES)),
            *pairs(CHUNKS),
        ],
        compiler_params=pltpu.CompilerParams(
            collective_id=0, has_side_effects=True, vmem_limit_bytes=56 * 2**20
        ),
        cost_estimate=pl.CostEstimate(
            flops=2 * 1024 * WIDE * CHUNKS * DEEP, bytes_accessed=8 * 2**20, transcendentals=0
        ),
    )(amplitudes, integral_slab, allowed_slots, row_energy[None, :], col_row[:, None])


def solution(mesh):
    placed = (
        P("rep", "orb", None),
        P("rep", None, "orb"),
        P(None, "rep"),
        P("orb"),
        P(None, "rep"),
    )
    return jax.shard_map(
        per_device, mesh=mesh, in_specs=placed, out_specs=P("rep", "orb"), check_vma=False
    )
```

```python
import jax
import jax.numpy as jnp
from jax import lax
from jax.experimental import pallas as pl
from jax.experimental.pallas import tpu as pltpu
from jax.sharding import PartitionSpec as P

IRREPS = 8
MESH = pl.DeviceIdType.MESH

Y, Z, CORES = 4, 8, 2
ORB = Y * Z * CORES
REP = 4
LINE = 4
QUARTERS = 4
SOURCES = ORB // QUARTERS
TARGETS = ORB // 2
SLOTS_OWN = 44
PACK = 16
THIRDS = 3
CHUNKS = 8
FULL = 6
NARROW = 128
WIDE = 2 * NARROW
BLOCK = CHUNKS * NARROW
COLS_OWN = 128
COLS_OUT = 256
HALF = COLS_OUT // 2
OPPOSITE, OWN, BESIDE = 0, 3, (1, 2)
QUARTER = THIRDS * SOURCES * PACK
DEEP = 2 * QUARTER
ROWS_Y = Z * CORES * SLOTS_OWN
COLUMNS = Z * CORES * THIRDS * PACK
PIECES = [(chunk, pl.ds(0, WIDE)) for chunk in range(CHUNKS - 1)]
PIECES += [(CHUNKS - 1, pl.ds(0, NARROW)), (CHUNKS - 1, pl.ds(NARROW, NARROW))]
SENT_AFTER = {piece: (piece + 3,) for piece in range(CHUNKS - 2)}


def transfer(src, dst, send_sem, recv_sem, orb, rep):
    return pltpu.make_async_remote_copy(
        src_ref=src,
        dst_ref=dst,
        send_sem=send_sem,
        recv_sem=recv_sem,
        device_id=(orb, rep),
        device_id_type=MESH,
    )


def settle(ref, sem):
    pltpu.make_async_copy(ref, ref, sem).wait()


def kernel(
    amp, integrals, allowed, row_energy, col_energy, out,
    stage, packed, arrived, order, slab_own, slab, part, near, summed, both, cross,
    stage_sem, amp_send, amp_recv, line_send, line_recv, pair_send, pair_recv,
    near_recv, rep_send, rep_recv, cross_send, cross_recv,
):
    me = lax.axis_index("orb")
    rep = lax.axis_index("rep")
    y, z, core = me // (Z * CORES), (me // CORES) % Z, me % CORES
    low, high = z % LINE, z // LINE
    upper = low // 2
    sibling = me + 1 - 2 * core
    partner = me + 2 * CORES - 4 * CORES * upper

    def device(y, z, core):
        return y * (Z * CORES) + z * CORES + core

    def target(turn):
        kind, s = turn % 4, turn // 4
        near = kind % 2
        half = (1 - near) * (kind // 2) + near * (upper + (kind // 2) * (1 - 2 * upper))
        group = (high + 1 - near) % 2
        quarter = ((z - LINE * group + Z + 3) // 2) % QUARTERS
        place = (quarter - half + LINE) % LINE
        to_y = (y + s + kind + 2) % Y
        to_core = (core + 1 - s // 4) % CORES
        return to_y, group, place, to_core, half

    def target_id(turn):
        to_y, group, place, to_core, _ = target(turn)
        return device(to_y, group * LINE + place, to_core)

    def first_rows(turn):
        to_y, group, place, to_core, _ = target(turn)
        return device(to_y, group * LINE + place % 2, to_core)

    def load(turn, side):
        base = pl.multiple_of((first_rows(turn) + side * 2 * CORES) * BLOCK, BLOCK)
        return pltpu.make_async_copy(
            amp.at[0, :, pl.ds(base, BLOCK)], stage.at[turn, side], stage_sem.at[turn, side]
        )

    @pl.loop(0, TARGETS)
    def _(turn):
        load(turn, 0).start()
        load(turn, 1).start()

    barrier = pltpu.get_barrier_semaphore()

    @pl.loop(0, TARGETS)
    def _(index):
        step = index // (Y * CORES)
        from_z = (LINE * high + 2 * low - 3 + step + Z) % Z
        source = device((index // CORES) % Y, from_z, index % CORES)

        @pl.when(source != me)
        def _():
            pl.semaphore_signal(barrier, inc=1, device_id=(source, rep), device_id_type=MESH)

    for step in range(1, REP):
        pl.semaphore_signal(
            barrier, inc=1, device_id=(me, (rep + step) % REP), device_id_type=MESH
        )
    for step in range(1, LINE):
        pl.semaphore_signal(
            barrier, inc=1,
            device_id=(me + CORES * ((low + step) % LINE - low), rep), device_id_type=MESH,
        )
    pl.semaphore_signal(barrier, inc=1, device_id=(sibling, rep), device_id_type=MESH)
    pl.semaphore_wait(barrier, TARGETS - 1 + REP - 1 + LINE - 1 + 1)

    own = low * CORES + core

    def quarter_of(place, half):
        quarter = (place + half + 2 + 2 * high) % QUARTERS
        return pl.ds(pl.multiple_of(quarter * QUARTER, QUARTER), QUARTER)

    def order_slab():
        across = lax.broadcasted_iota(jnp.int32, (1, COLUMNS), 1)
        piece, within = across // 64, across % 64
        slot = piece % THIRDS * PACK + within % PACK
        from_z = (2 * (piece // THIRDS) + 1 + within // 32) % Z
        row = (from_z * CORES + within // PACK % CORES) * SLOTS_OWN + slot
        row = jnp.where(slot < SLOTS_OWN, row, -1)
        down = lax.broadcasted_iota(jnp.int32, (ROWS_Y, COLUMNS), 0)
        order[...] = jnp.where(down == row, 1.0, 0.0).astype(jnp.bfloat16)
        irrep = lax.broadcasted_iota(jnp.int32, (IRREPS, COLUMNS), 0)
        for at_y in range(Y):
            rows = slice(at_y * ROWS_Y, (at_y + 1) * ROWS_Y)
            live = lax.dot_general(
                integrals[0, rows], order[...], (((0,), (0,)), ((), ())),
                preferred_element_type=jnp.float32,
            )
            mask = jnp.dot(
                allowed[:, rows].astype(jnp.float32).astype(jnp.bfloat16), order[...],
                preferred_element_type=jnp.float32,
            )
            mask = jnp.sum(
                jnp.where(irrep == me // (ORB // IRREPS), mask, 0.0), axis=0, keepdims=True
            )
            live = (live * mask).astype(jnp.bfloat16)
            for piece in range(QUARTERS * THIRDS):
                first = piece * SOURCES * PACK + at_y * 64
                slab_own[:, first:first + 64] = live[:, piece * 64:(piece + 1) * 64]

    def to_sibling(step):
        at = (low - step + LINE) % LINE * CORES + core
        return transfer(
            slab.at[at], slab.at[at], pair_send.at[step], pair_recv.at[step], sibling, rep
        )

    def send_slab(step, half):
        place = (low + step) % LINE
        transfer(
            slab_own.at[:, quarter_of(place, half)],
            slab.at[own, :, pl.ds(half * QUARTER, QUARTER)],
            line_send.at[step - 1], line_recv.at[step - 1], me + CORES * (place - low), rep,
        ).start()

    def pack(turn, store):
        for side in range(2):
            load(turn, side).wait()
            lanes = slice(side * NARROW, (side + 1) * NARROW)

            def read(first, last, chunk):
                return stage[turn, side, first:last, chunk * NARROW:(chunk + 1) * NARROW]

            lasts = [read(32, SLOTS_OWN, chunk).astype(jnp.float32) for chunk in range(FULL, CHUNKS)]
            for chunk in range(CHUNKS):
                store(chunk, 0, lanes, read(0, 16, chunk))
                store(chunk, 1, lanes, read(16, 32, chunk))
                if chunk < FULL:
                    rest = read(32, SLOTS_OWN, chunk).astype(jnp.float32)
                    at = 4 * (chunk % 3)
                    tail = jnp.concatenate([rest, lasts[chunk // 3][at:at + 4]], axis=0)
                    store(chunk, 2, lanes, tail.astype(jnp.bfloat16))

    source_at = y * (2 * CORES) + (z + 1) % 2 * CORES + core

    def thirds(chunk):
        return pl.ds(0, THIRDS if chunk < FULL else 2)

    def send_block(piece, turn):
        chunk, lanes = PIECES[piece]
        half = target(turn)[-1]
        transfer(
            packed.at[chunk, turn, thirds(chunk), :, lanes],
            arrived.at[chunk, half, thirds(chunk), source_at, :, lanes],
            amp_send.at[piece], amp_recv.at[piece], target_id(turn), rep,
        ).start()

    def send_piece(piece, first=0, last=TARGETS - 1):
        @pl.loop(first, last)
        def _(turn):
            send_block(piece, turn)

    def sent(piece):
        chunk, lanes = PIECES[piece]
        return packed.at[chunk, pl.ds(0, TARGETS - 1), thirds(chunk), :, lanes]

    @pl.loop(0, TARGETS - 1)
    def _(turn):
        def store(chunk, third, lanes, value):
            packed[chunk, turn, third, :, lanes] = value

        pack(turn, store)
        send_block(0, turn)

    def store_own(chunk, third, lanes, value):
        arrived[chunk, 1 - upper, third, source_at, :, lanes] = value

    pack(TARGETS - 1, store_own)
    order_slab()
    for part_of in range(6):
        send_slab(1 + part_of % 3, part_of // 3)
        send_piece(1, part_of * 5, part_of * 5 + 5 if part_of < 5 else TARGETS - 1)
    for half in range(2):
        slab[own, :, half * QUARTER:(half + 1) * QUARTER] = slab_own[:, quarter_of(low, half)]
    to_sibling(0).start()
    send_piece(2)
    for step in range(1, LINE):
        at = (low - step + LINE) % LINE * CORES + core
        settle(slab.at[at], line_recv.at[step - 1])
        to_sibling(step).start()
    for step in range(LINE):
        settle(slab.at[own], pair_recv.at[step])

    def to_side(piece, way, src, dst, sem):
        return transfer(
            src, dst, rep_send.at[piece], sem, me, (rep + 1 + 2 * way) % REP
        )

    def half_rows(way):
        return pl.ds(way * HALF, HALF)

    def through(piece, way):
        chunk, lanes = PIECES[piece]
        return to_side(
            piece, way, part.at[chunk, OPPOSITE, half_rows(way), lanes],
            near.at[chunk, way, :, lanes], near_recv.at[piece],
        )

    def direct(piece, way, half):
        chunk, lanes = PIECES[piece]
        rows = half_rows(half)
        return to_side(
            piece, way, part.at[chunk, BESIDE[way], rows, lanes],
            summed.at[chunk, way, rows, lanes], rep_recv.at[piece],
        )

    def contract(piece):
        chunk, lanes = PIECES[piece]

        @pl.loop(0, REP)
        def _(step):
            block = (rep + 2 + 3 * step + 3 * (step // 2) + 2 * (step // 3)) % REP
            rows = slab[pl.ds(block * 2, 2)].reshape(COLS_OUT, DEEP)
            part[chunk, step, :, lanes] = jnp.dot(
                rows,
                arrived[chunk, :, :, :, :, lanes].reshape(DEEP, lanes.size),
                preferred_element_type=jnp.float32,
            )

            @pl.when(step == OPPOSITE)
            def _():
                through(piece, 0).start()
                through(piece, 1).start()

            for way in range(2):

                @pl.when(step == BESIDE[way])
                def _():
                    direct(piece, way, 1 - way).start()

    def pass_on(piece):
        chunk, lanes = PIECES[piece]
        settle(near.at[chunk, :, :, lanes], near_recv.at[piece])
        for way in range(2):
            part[chunk, BESIDE[way], half_rows(way), lanes] += near[chunk, way, :, lanes]
            direct(piece, way, way).start()

    own_lanes = pl.ds(pl.multiple_of(upper * NARROW, NARROW), NARROW)
    other_lanes = pl.ds(pl.multiple_of((1 - upper) * NARROW, NARROW), NARROW)

    def to_partner(chunk):
        return transfer(
            both.at[chunk, :, other_lanes], cross.at[chunk],
            cross_send.at[chunk], cross_recv.at[chunk], partner, rep,
        )

    def sum_quarters(piece):
        chunk, lanes = PIECES[piece]
        settle(summed.at[chunk, :, :, lanes], rep_recv.at[piece])
        total = part[chunk, OWN, :, lanes] + summed[chunk, 0, :, lanes]
        both[chunk, :, lanes] = total + summed[chunk, 1, :, lanes]
        if lanes.size == WIDE:
            to_partner(chunk).start()
        else:

            @pl.when(upper == 1 - lanes.start // NARROW)
            def _():
                to_partner(chunk).start()

    def finish(chunk):
        to_partner(chunk).wait_recv()
        columns = slice(chunk * NARROW, (chunk + 1) * NARROW)
        total = both[chunk, :, own_lanes] + cross[chunk]
        out[:, columns] = total / (col_energy[...] + row_energy[:, columns])

    def gather_tail(chunk):
        rows = 2 * SOURCES * PACK
        place = lax.broadcasted_iota(jnp.int32, (rows, WIDE), 0) % PACK
        first = (chunk - FULL) * 3
        tails = [
            pltpu.roll(
                arrived[first + i, :, 2].reshape(rows, WIDE).astype(jnp.float32),
                rows - 12 + 4 * i,
                0,
            )
            for i in range(3)
        ]
        tail = jnp.where(place < 4, tails[0], jnp.where(place < 8, tails[1], tails[2]))
        arrived[chunk, :, 2] = tail.astype(jnp.bfloat16).reshape(2, SOURCES, PACK, WIDE)

    middle = TARGETS // 2
    done = 0
    for piece, (chunk, _) in enumerate(PIECES):
        settle(sent(piece), amp_recv.at[piece])
        for later in SENT_AFTER.get(piece, ()):
            send_piece(later, 0, middle)
        contract(piece)
        if piece >= 1:
            sum_quarters(piece - 1)
        if piece == 2:
            gather_tail(FULL)
        if piece == 5:
            gather_tail(FULL + 1)
        pass_on(piece)
        for later in SENT_AFTER.get(piece, ()):
            send_piece(later, middle, TARGETS - 1)
        while done < PIECES[piece - 1][0] and piece >= 2:
            finish(done)
            done += 1
    sum_quarters(len(PIECES) - 1)
    for chunk in range(done, CHUNKS):
        finish(chunk)

    for piece, (chunk, lanes) in enumerate(PIECES):
        settle(sent(piece), amp_send.at[piece])
        settle(part.at[chunk, pl.ds(0, REP - 1), :, lanes], rep_send.at[piece])
    for chunk in range(CHUNKS):
        to_partner(chunk).wait_send()
    for step in range(LINE - 1):
        settle(slab.at[own], line_send.at[step])
    for step in range(LINE):
        settle(slab.at[own], pair_send.at[step])


def per_device(amplitudes, integral_slab, allowed_slots, row_energy, col_energy):
    irrep_index = lax.axis_index("orb") // (lax.axis_size("orb") // IRREPS)
    col_row = lax.dynamic_slice_in_dim(col_energy, irrep_index, 1, 0)[0]
    vmem = pl.BlockSpec(memory_space=pltpu.VMEM)
    pairs = lambda count: [pltpu.SemaphoreType.DMA((count,))] * 2
    return pl.pallas_call(
        kernel,
        out_shape=jax.ShapeDtypeStruct((COLS_OUT, BLOCK), jnp.float32),
        in_specs=[pl.BlockSpec(memory_space=pl.ANY)] + [vmem] * 4,
        out_specs=vmem,
        scratch_shapes=[
            pltpu.VMEM((TARGETS, 2, SLOTS_OWN, BLOCK), jnp.bfloat16),
            pltpu.VMEM((CHUNKS, TARGETS, THIRDS, PACK, WIDE), jnp.bfloat16),
            pltpu.VMEM((CHUNKS, 2, THIRDS, SOURCES, PACK, WIDE), jnp.bfloat16),
            pltpu.VMEM((ROWS_Y, COLUMNS), jnp.bfloat16),
            pltpu.VMEM((COLS_OWN, QUARTERS * QUARTER), jnp.bfloat16),
            pltpu.VMEM((LINE * CORES, COLS_OWN, DEEP), jnp.bfloat16),
            pltpu.VMEM((CHUNKS, REP, COLS_OUT, WIDE), jnp.float32),
            pltpu.VMEM((CHUNKS, 2, HALF, WIDE), jnp.float32),
            pltpu.VMEM((CHUNKS, 2, COLS_OUT, WIDE), jnp.float32),
            pltpu.VMEM((CHUNKS, COLS_OUT, WIDE), jnp.float32),
            pltpu.VMEM((CHUNKS, COLS_OUT, NARROW), jnp.float32),
            pltpu.SemaphoreType.DMA((TARGETS, 2)),
            *pairs(len(PIECES)),
            *pairs(LINE - 1),
            *pairs(LINE),
            pltpu.SemaphoreType.DMA((len(PIECES),)),
            *pairs(len(PIECES)),
            *pairs(CHUNKS),
        ],
        compiler_params=pltpu.CompilerParams(
            collective_id=0, has_side_effects=True, vmem_limit_bytes=56 * 2**20
        ),
        cost_estimate=pl.CostEstimate(
            flops=2 * 1024 * WIDE * CHUNKS * DEEP, bytes_accessed=8 * 2**20, transcendentals=0
        ),
    )(amplitudes, integral_slab, allowed_slots, row_energy[None, :], col_row[:, None])


def solution(mesh):
    placed = (
        P("rep", "orb", None),
        P("rep", None, "orb"),
        P(None, "rep"),
        P("orb"),
        P(None, "rep"),
    )
    return jax.shard_map(
        per_device, mesh=mesh, in_specs=placed, out_specs=P("rep", "orb"), check_vma=False
    )
```
